32 devices in a mesh: seq: 8 (over z, x), dp: 4 (over y, core).
Axes of the slice: x: 2, y: 2, z: 4, core: 2. Of those that a mesh axis runs over, the one named last changes fastest.
Arguments:
- emb_grad: bfloat16 [4, 8192, 1792], P('dp', 'seq'), may hold values from -6 to 6
- image_map: int32 [4, 8192], P('dp', 'seq'), may hold values from -1 to 8191, as said below
- pre_act: bfloat16 [4, 8192, 2560], P('dp', 'seq'), may hold values from -8 to 8
- w_down: bfloat16 [2560, 1792], P('seq'), may hold values from -0.125 to 0.125
Outputs:
- act_grad: bfloat16 [4, 8192, 2560], P('dp', 'seq')
- w_grad: float32 [2560, 1792], P('seq')
The draws below stay inside these ranges and needn't reach their ends.
Inputs may be any that keep to these rules, and one draw needn't show every extreme that they name: `image_map`: no two tokens of one replica name the same row. The tokens of one device name at most 128 rows of one device's block of 1024 rows; in every draw some device's block gets exactly 128 rows from every device. Loads of the blocks are skewed.
All inputs are finite; a program needn't handle non-finite values.
Results may differ from the reference program's by a relative error of at most 0.0026.
Values may be sent and summed in bfloat16 or wider, within the bound.
No kernel may reach another device: no remote copies, remote signals or barrier semaphores. Data moves between devices by JAX's collectives and lax.ppermute only.
A program may use at most 128 MiB of HBM per device.

```python
import math
import jax
import jax.numpy as jnp
from jax import lax

D = 1792
HID = 2560
TOK_DEV = 1024
REPL = 4
TOKENS = 8192
ROWS = 8192
CAP = 128
N_SEQ = 8
N_DP = 4


def map_for_replica(key):
    subkeys = jax.random.split(key, 5)
    levels = jax.random.randint(subkeys[0], (N_SEQ,), 0, CAP + 1)
    full_dev = jax.random.randint(subkeys[1], (), 0, N_SEQ)
    raw_counts = jax.random.randint(subkeys[2], (N_SEQ, N_SEQ), 0, CAP + 1)
    counts = jnp.minimum(raw_counts, levels[None, :])
    counts = jnp.where(jnp.arange(N_SEQ)[None, :] == full_dev, CAP, counts)
    before = jnp.cumsum(counts, axis=0) - counts
    slot_dev = jnp.arange(TOK_DEV) // CAP
    slot_rank = jnp.arange(TOK_DEV) % CAP
    is_valid = slot_rank[None, :] < counts[:, slot_dev]
    incoming = before[:, slot_dev] + slot_rank[None, :]
    row_perm = jax.vmap(lambda sub: jax.random.permutation(sub, TOK_DEV))(jax.random.split(subkeys[3], N_SEQ))
    row_pick = row_perm[slot_dev[None, :], jnp.minimum(incoming, TOK_DEV - 1)]
    targets = jnp.where(is_valid, slot_dev[None, :] * TOK_DEV + row_pick, -1).astype(jnp.int32)
    tok_perm = jax.vmap(lambda sub: jax.random.permutation(sub, TOK_DEV))(jax.random.split(subkeys[4], N_SEQ))
    result = jnp.full((N_SEQ, TOK_DEV), -1, jnp.int32)
    result = result.at[jnp.arange(N_SEQ)[:, None], tok_perm].set(targets)
    return result.reshape(N_SEQ * TOK_DEV)


def draw_image_map(key, part):
    subkeys = jax.random.split(jax.random.fold_in(key, 7), N_DP)
    return jax.vmap(map_for_replica)(subkeys)


def level_of(key, extent, shards, smallest, high):
    factor_of, own = 1.0, jax.random.fold_in(key, 6)
    for axis_at, parts in shards:
        heights = jnp.exp(jax.random.uniform(jax.random.fold_in(own, axis_at), (parts,), jnp.float32, smallest / len(shards), high / len(shards)))
        factor_of = factor_of * jnp.repeat(heights, extent[axis_at] // parts).reshape([-1 if axis == axis_at else 1 for axis in range(len(extent))])
    return factor_of


def scatter_about(own_key, extent, width, reach, cuts=(), kind=jnp.bfloat16):
    values = width * jax.random.normal(own_key, extent, jnp.float32)
    if cuts:
        values = values * level_of(own_key, extent, cuts, -0.22, 0.18)
    return jnp.clip(values, -reach, reach).astype(kind)


def setup_inputs(seed: int = 0) -> dict:
    arg_keys = jax.random.split(jax.random.key(seed), 5)
    return {
        "emb_grad": scatter_about(arg_keys[0], (REPL, TOKENS, D), 1.0, 6.0, ((0, 4), (1, 8))),
        "image_map": draw_image_map(jax.random.fold_in(arg_keys[4], 71), 0),
        "pre_act": scatter_about(arg_keys[2], (REPL, ROWS, HID), 1.5, 8.0, ((0, 4), (1, 8))),
        "w_down": scatter_about(arg_keys[3], (HID, D), HID ** -0.5, 0.125, ((0, 8),)),
    }


def gelu_parts(pre_rows):
    values = pre_rows.astype(jnp.float32)
    normal_cdf = 0.5 * (1.0 + lax.erf(values * (1.0 / math.sqrt(2.0))))
    density = jnp.exp(-0.5 * values * values) * (1.0 / math.sqrt(2.0 * math.pi))
    return (values * normal_cdf, normal_cdf + values * density)

def one_replica(token_grad, targets, pre_rows, w_down):
    row_total = pre_rows.shape[0]
    segment = jnp.where(targets < 0, row_total, targets).astype(jnp.int32)
    placed = jax.ops.segment_sum(token_grad.astype(jnp.float32), segment, num_segments=row_total + 1)[:row_total].astype(jnp.bfloat16)
    activation, gelu_slope = gelu_parts(pre_rows)
    hidden_grad = lax.dot_general(placed, w_down, (((1,), (1,)), ((), ())), preferred_element_type=jnp.float32)
    act_grad = (hidden_grad * gelu_slope).astype(jnp.bfloat16)
    hidden = activation.astype(jnp.bfloat16)
    partial_value = lax.dot_general(hidden, placed, (((0,), (0,)), ((), ())), preferred_element_type=jnp.float32)
    return (act_grad, partial_value)

def reference(emb_grad, image_map, pre_act, w_down):
    replicas = emb_grad.shape[0]
    grads = []
    grad_total = jnp.zeros((w_down.shape[0], w_down.shape[1]), jnp.float32)
    for index in range(replicas):
        act_grad, partial_value = one_replica(emb_grad[index], image_map[index], pre_act[index], w_down)
        grads.append(act_grad)
        grad_total = grad_total + partial_value
    normalizer = 1.0 / math.sqrt(replicas * pre_act.shape[1])
    return (jnp.stack(grads, axis=0), grad_total * normalizer)
```

```python
import functools
import math

import jax
import jax.numpy as jnp
from jax import lax
from jax.experimental import pallas as pl
from jax.experimental.pallas import tpu as pltpu
from jax.sharding import PartitionSpec as P

F32, BF16, I32 = jnp.float32, jnp.bfloat16, jnp.int32
MIB = 2**20
WIDTHS = (256, 512, 512, 256, 256)
ID_BASE = 32
ID_ROWS = 16
GROUP = 640


def dot(a, b, dims=((1,), (0,))):
    return lax.dot_general(a, b, (dims, ((), ())), preferred_element_type=F32)


def params(mib):
    return pltpu.CompilerParams(vmem_limit_bytes=mib * MIB)


def cost(flops, nbytes):
    return pl.CostEstimate(flops=int(flops), bytes_accessed=int(nbytes), transcendentals=0)


def whole(*dims):
    return pl.BlockSpec(dims, lambda *_: (0,) * len(dims))


def reverse(index, bits):
    back = 0
    for bit in range(bits):
        one = lax.bitwise_and(lax.shift_right_logical(index, bit), 1)
        back = back + one * (1 << (bits - 1 - bit))
    return back


def route_kernel(n_seq, cap, rows_dev, map_ref, emb_ref, pick_ref, send_ref):
    targets = map_ref[...]
    groups, lanes = targets.shape
    live = targets >= 0
    safe = jnp.where(live, targets, 0)
    owner = jnp.where(live, lax.div(safe, rows_dev), n_seq)
    members = [(owner == j).astype(F32) for j in range(n_seq)]
    table = jnp.concatenate(members, axis=0).astype(BF16)
    upper = (
        lax.broadcasted_iota(I32, (lanes, lanes), 0) < lax.broadcasted_iota(I32, (lanes, lanes), 1)
    ).astype(F32).astype(BF16)
    inside = dot(table, upper)
    total = n_seq * groups
    row = lax.broadcasted_iota(I32, (total, total), 0)
    col = lax.broadcasted_iota(I32, (total, total), 1)
    earlier = ((lax.div(row, groups) == lax.div(col, groups)) & (col < row)).astype(F32).astype(BF16)
    counts = dot(table, jnp.ones((lanes, lanes), BF16))
    rank_all = inside + dot(earlier, counts.astype(BF16))
    rank = jnp.zeros((groups, lanes), F32)
    for j in range(n_seq):
        rank = rank + members[j] * rank_all[j * groups : (j + 1) * groups]
    slot = jnp.where(live, owner * cap + rank.astype(I32), -1)
    number = jnp.where(live, safe - owner * rows_dev + 1, 0)
    high = lax.div(number, ID_BASE)
    low = (number - high * ID_BASE).astype(F32).astype(BF16)
    high = high.astype(F32).astype(BF16)
    slots = n_seq * cap
    place = lax.broadcasted_iota(I32, (slots, lanes), 0)
    ids = jnp.zeros((ID_ROWS, slots), F32)
    for g in range(groups):
        part = (place == slot[g : g + 1]).astype(F32).astype(BF16)
        pick_ref[:, g * lanes : (g + 1) * lanes] = part
        pair = jnp.concatenate(
            [
                jnp.broadcast_to(high[g : g + 1], (ID_ROWS // 2, lanes)),
                jnp.broadcast_to(low[g : g + 1], (ID_ROWS // 2, lanes)),
            ],
            axis=0,
        )
        ids = ids + dot(pair, part, ((1,), (1,)))
    ids = ids.astype(BF16)
    moved = dot(pick_ref[...], emb_ref[...]).astype(BF16)
    width = emb_ref.shape[1]
    for j in range(n_seq):
        send_ref[j, :cap] = moved[j * cap : (j + 1) * cap]
        digits = ids[:, j * cap : (j + 1) * cap]
        rest = jnp.zeros((ID_ROWS, width - cap), BF16)
        send_ref[j, cap:] = jnp.concatenate([digits, rest], axis=1)


def pack_kernel(n_seq, cap, start, widths, pick_ref, emb_ref, *send_refs):
    first = start
    for send_ref, width in zip(send_refs, widths):
        moved = dot(pick_ref[...], emb_ref[:, first : first + width]).astype(BF16)
        for j in range(n_seq):
            send_ref[j] = moved[j * cap : (j + 1) * cap]
        first += width


def hidden_kernel(height, me_ref, pre_ref, mine_ref, theirs_ref, slope_ref):
    values = pre_ref[...].astype(F32)
    normal_cdf = 0.5 * (1.0 + lax.erf(values * (1.0 / math.sqrt(2.0))))
    density = jnp.exp(-0.5 * values * values) * (1.0 / math.sqrt(2.0 * math.pi))
    slope_ref[...] = normal_cdf + values * density
    hidden = (values * normal_cdf).astype(BF16).T
    even_mine = lax.bitwise_and(me_ref[1], 1) == 0
    for k in range(mine_ref.shape[0] // height):
        even = hidden[2 * k * height : (2 * k + 1) * height]
        odd = hidden[(2 * k + 1) * height : (2 * k + 2) * height]
        mine_ref[k * height : (k + 1) * height] = jnp.where(even_mine, even, odd)
        theirs_ref[k * height : (k + 1) * height] = jnp.where(even_mine, odd, even)


def landing_kernel(n_seq, cap, rows_dev, got_ref, land_ref):
    lows = ID_ROWS // 2
    ids = []
    for i in range(n_seq):
        digits = got_ref[i, cap:].astype(F32)[:, :cap]
        ids.append(digits[0:1] * float(ID_BASE) + digits[lows : lows + 1])
    ids = jnp.concatenate(ids, axis=1).astype(I32) - 1
    slots = ids.shape[1]
    step = 128
    for first in range(0, rows_dev, step):
        row = lax.broadcasted_iota(I32, (step, slots), 0) + first
        land_ref[first : first + step] = (row == ids).astype(F32).astype(BF16)


def place_kernel(n_seq, cap, n_after, land_ref, got_ref, *refs):
    placed_ref = refs[n_after]
    got = jnp.concatenate([got_ref[i, :cap] for i in range(n_seq)], axis=0)
    placed_ref[...] = dot(land_ref[...], got).astype(BF16)


def share_kernel(n_seq, n_pairs, height, me_ref, mine_ref, theirs_ref, own_ref, other_ref, away_ref, keep_ref):
    step = pl.program_id(0)
    share = dot(mine_ref[...], own_ref[...]) + dot(theirs_ref[...], other_ref[...])
    bits = n_seq.bit_length() - 1
    my_pair = lax.shift_right_logical(me_ref[1], 1)
    per_step = mine_ref.shape[0] // (height * n_pairs)
    half = n_pairs // 2
    for a in range(per_step):
        u = reverse(lax.bitwise_xor(step * per_step + a, me_ref[0]), bits)
        for p in range(half):
            low = (a * n_pairs + p) * height
            high = (a * n_pairs + p + half) * height
            low, high = share[low : low + height], share[high : high + height]
            low_mine = my_pair < half
            at = lax.bitwise_xor(p, lax.bitwise_and(my_pair, half - 1)) * n_seq + u
            keep_ref[at] = jnp.where(low_mine, low, high)
            away_ref[at] = jnp.where(low_mine, high, low).astype(BF16)


def act_kernel(n_pieces, n_parts, me_ref, *refs):
    placed_refs, refs = refs[:n_parts], refs[n_parts:]
    mine_refs, refs = refs[:n_pieces], refs[n_pieces:]
    their_refs, refs = refs[:n_pieces], refs[n_pieces:]
    slope_ref, out_ref = refs[0], refs[-1]
    even_mine = lax.bitwise_and(me_ref[1], 1) == 0
    blocks = []
    for mine, theirs in zip(mine_refs, their_refs):
        blocks.append(jnp.where(even_mine, mine[0], theirs[0]))
        blocks.append(jnp.where(even_mine, theirs[0], mine[0]))
    weights = jnp.concatenate(blocks, axis=0)
    placed = jnp.concatenate([r[...] for r in placed_refs], axis=1)
    grad = dot(placed, weights, ((1,), (1,)))
    out_ref[...] = (grad * slope_ref[...]).astype(BF16)


def swap(value, axis, bit):
    size = lax.axis_size(axis)
    return lax.ppermute(value, axis, [(i, i ^ (1 << bit)) for i in range(size)])


def local(emb_grad, image_map, pre_act, w_down):
    n_seq, n_dp = lax.axis_size("seq"), lax.axis_size("dp")
    seq_bits, dp_bits = n_seq.bit_length() - 1, n_dp.bit_length() - 1
    me_s = lax.axis_index("seq").astype(I32)
    me_d = lax.axis_index("dp").astype(I32)
    me = jnp.stack([me_s, me_d])
    tokens, dim = emb_grad.shape[1:]
    rows_dev, hid = pre_act.shape[1:]
    cap = rows_dev // n_seq
    slots = n_seq * cap
    emb, pre = emb_grad[0], pre_act[0]
    n_parts = len(WIDTHS)
    height = hid // (n_seq * n_dp)
    smem = pl.BlockSpec(memory_space=pltpu.SMEM)
    anywhere = pl.BlockSpec(memory_space=pl.ANY)
    shape = jax.ShapeDtypeStruct

    weights = lax.dynamic_slice(w_down, (me_d * height, 0), (height, dim))[None]
    for bit in reversed(range(seq_bits)):
        weights = jnp.concatenate([weights, swap(weights, "seq", bit)], axis=0)
    for bit in reversed(range(1, dp_bits)):
        weights = jnp.concatenate([weights, swap(weights, "dp", bit)], axis=0)
    their_weights = swap(weights, "dp", 0)

    def exchange(blocks):
        return lax.all_to_all(blocks, "seq", split_axis=0, concat_axis=0, tiled=True)

    pick, sends = pl.pallas_call(
        functools.partial(route_kernel, n_seq, cap, rows_dev),
        grid=(1,),
        in_specs=[whole(tokens // 128, 128), whole(tokens, WIDTHS[0])],
        out_specs=[whole(slots, tokens), whole(n_seq, cap + ID_ROWS, WIDTHS[0])],
        out_shape=[
            shape((slots, tokens), BF16),
            shape((n_seq, cap + ID_ROWS, WIDTHS[0]), BF16),
        ],
        compiler_params=params(20),
        cost_estimate=cost(4e9, 4e6),
        name="route",
    )(image_map.reshape(tokens // 128, 128), emb)
    got_parts = [exchange(sends)]

    rest = WIDTHS[1:]
    packed = pl.pallas_call(
        functools.partial(pack_kernel, n_seq, cap, WIDTHS[0], rest),
        grid=(1,),
        in_specs=[whole(slots, tokens), whole(tokens, dim)],
        out_specs=[whole(n_seq, cap, w) for w in rest],
        out_shape=[shape((n_seq, cap, w), BF16) for w in rest],
        compiler_params=params(40),
        cost_estimate=cost(4e9, 8e6),
        name="pack",
    )(pick, emb)
    got_parts += [exchange(p) for p in packed]

    mine_t, away_t, slope = pl.pallas_call(
        functools.partial(hidden_kernel, height),
        grid=(hid // GROUP,),
        in_specs=[smem, pl.BlockSpec((rows_dev, GROUP), lambda i: (0, i))],
        out_specs=[pl.BlockSpec((GROUP // 2, rows_dev), lambda i: (i, 0))] * 2
        + [pl.BlockSpec((rows_dev, GROUP), lambda i: (0, i))],
        out_shape=[shape((hid // 2, rows_dev), BF16)] * 2 + [shape((rows_dev, hid), F32)],
        compiler_params=params(40),
        cost_estimate=cost(4e9, 21e6),
        name="hidden",
    )(me, pre)
    theirs_t = swap(away_t, "dp", 0)
    land = pl.pallas_call(
        functools.partial(landing_kernel, n_seq, cap, rows_dev),
        grid=(1,),
        in_specs=[whole(n_seq, cap + ID_ROWS, WIDTHS[0])],
        out_specs=whole(rows_dev, slots),
        out_shape=shape((rows_dev, slots), BF16),
        compiler_params=params(16),
        cost_estimate=cost(1e9, 3e6),
        name="landing",
    )(got_parts[0])

    normalizer = 1.0 / math.sqrt(n_dp * rows_dev * n_seq)
    n_pairs = n_dp // 2
    kept = n_seq * n_pairs // 2
    placed_parts, grads = [], []
    for c in range(n_parts):
        width = WIDTHS[c]
        got = got_parts[c]
        after = []
        placed = pl.pallas_call(
            functools.partial(place_kernel, n_seq, cap, len(after)),
            grid=(1,),
            in_specs=[whole(rows_dev, slots), whole(*got.shape)] + [anywhere] * len(after),
            out_specs=whole(rows_dev, width),
            out_shape=shape((rows_dev, width), BF16),
            compiler_params=params(16),
            cost_estimate=cost(2 * rows_dev * width * slots, 4e6),
            name="place",
        )(land, got, *after)
        placed_parts.append(placed)
        other = swap(placed, "dp", 0)
        away, keep = pl.pallas_call(
            functools.partial(share_kernel, n_seq, n_pairs, height),
            grid=(hid // GROUP,),
            in_specs=[smem]
            + [pl.BlockSpec((GROUP // 2, rows_dev), lambda i: (i, 0))] * 2
            + [whole(rows_dev, width)] * 2,
            out_specs=[whole(kept, height, width)] * 2,
            out_shape=[shape((kept, height, width), BF16), shape((kept, height, width), F32)],
            compiler_params=params(24),
            cost_estimate=cost(2 * rows_dev * width * hid, 8e6),
            name="share",
        )(me, mine_t, theirs_t, placed, other)
        total = keep + swap(away, "dp", dp_bits - 1).astype(F32)
        order = [("dp", bit) for bit in reversed(range(1, dp_bits - 1))]
        order += [("seq", bit) for bit in range(seq_bits)]
        for axis, bit in order:
            n = total.shape[0] // 2
            total = total[:n] + swap(total[n:].astype(BF16), axis, bit).astype(F32)
        grads.append(lax.all_gather(total[0] * normalizer, "dp", axis=0, tiled=True))

    n_pieces = GROUP // (2 * height)

    def w_spec(k):
        def index(i, me_ref):
            flat = i * n_pieces + k
            s, pair = lax.div(flat, n_pairs), lax.rem(flat, n_pairs)
            u = lax.bitwise_xor(s, me_ref[0])
            v = lax.bitwise_xor(pair, lax.shift_right_logical(me_ref[1], 1))
            return (reverse(v, dp_bits - 1) * n_seq + reverse(u, seq_bits), 0, 0)

        return pl.BlockSpec((1, height, dim), index)

    act_grad = pl.pallas_call(
        functools.partial(act_kernel, n_pieces, n_parts),
        grid_spec=pltpu.PrefetchScalarGridSpec(
            num_scalar_prefetch=1,
            grid=(hid // GROUP,),
            in_specs=[whole(rows_dev, w) for w in WIDTHS]
            + [w_spec(k) for k in range(n_pieces)] * 2
            + [pl.BlockSpec((rows_dev, GROUP), lambda i, m: (0, i))],
            out_specs=pl.BlockSpec((rows_dev, GROUP), lambda i, m: (0, i)),
        ),
        out_shape=shape((rows_dev, hid), BF16),
        compiler_params=params(48),
        cost_estimate=cost(2 * rows_dev * dim * hid, 29e6),
        name="act",
    )(me, *placed_parts, *([weights] * n_pieces), *([their_weights] * n_pieces), slope)
    return act_grad[None], jnp.concatenate(grads, axis=1)


def solution(mesh):
    placed = (P("dp", "seq", None), P("dp", "seq"), P("dp", "seq", None), P("seq", None))
    return jax.shard_map(
        local,
        mesh=mesh,
        in_specs=placed,
        out_specs=(P("dp", "seq", None), P("seq", None)),
        check_vma=False,
    )
```

```python
import functools
import math

import jax
import jax.numpy as jnp
from jax import lax
from jax.experimental import pallas as pl
from jax.experimental.pallas import tpu as pltpu
from jax.sharding import PartitionSpec as P

F32, BF16, I32 = jnp.float32, jnp.bfloat16, jnp.int32
MIB = 2**20
WIDTHS = (1280, 512)
ID_BASE = 32
ID_ROWS = 16
GROUP = 640


def dot(a, b, dims=((1,), (0,))):
    return lax.dot_general(a, b, (dims, ((), ())), preferred_element_type=F32)


def params(mib):
    return pltpu.CompilerParams(vmem_limit_bytes=mib * MIB)


def cost(flops, nbytes):
    return pl.CostEstimate(flops=int(flops), bytes_accessed=int(nbytes), transcendentals=0)


def whole(*dims):
    return pl.BlockSpec(dims, lambda *_: (0,) * len(dims))


def reverse(index, bits):
    back = 0
    for bit in range(bits):
        one = lax.bitwise_and(lax.shift_right_logical(index, bit), 1)
        back = back + one * (1 << (bits - 1 - bit))
    return back


def route_kernel(n_seq, cap, rows_dev, map_ref, emb_ref, pick_ref, send_ref):
    targets = map_ref[...]
    groups, lanes = targets.shape
    live = targets >= 0
    safe = jnp.where(live, targets, 0)
    owner = jnp.where(live, lax.div(safe, rows_dev), n_seq)
    members = [(owner == j).astype(F32) for j in range(n_seq)]
    table = jnp.concatenate(members, axis=0).astype(BF16)
    upper = (
        lax.broadcasted_iota(I32, (lanes, lanes), 0) < lax.broadcasted_iota(I32, (lanes, lanes), 1)
    ).astype(F32).astype(BF16)
    inside = dot(table, upper)
    total = n_seq * groups
    row = lax.broadcasted_iota(I32, (total, total), 0)
    col = lax.broadcasted_iota(I32, (total, total), 1)
    earlier = ((lax.div(row, groups) == lax.div(col, groups)) & (col < row)).astype(F32).astype(BF16)
    counts = dot(table, jnp.ones((lanes, lanes), BF16))
    rank_all = inside + dot(earlier, counts.astype(BF16))
    rank = jnp.zeros((groups, lanes), F32)
    for j in range(n_seq):
        rank = rank + members[j] * rank_all[j * groups : (j + 1) * groups]
    slot = jnp.where(live, owner * cap + rank.astype(I32), -1)
    number = jnp.where(live, safe - owner * rows_dev + 1, 0)
    high = lax.div(number, ID_BASE)
    low = (number - high * ID_BASE).astype(F32).astype(BF16)
    high = high.astype(F32).astype(BF16)
    slots = n_seq * cap
    place = lax.broadcasted_iota(I32, (slots, lanes), 0)
    ids = jnp.zeros((ID_ROWS, slots), F32)
    for g in range(groups):
        part = (place == slot[g : g + 1]).astype(F32).astype(BF16)
        pick_ref[:, g * lanes : (g + 1) * lanes] = part
        pair = jnp.concatenate(
            [
                jnp.broadcast_to(high[g : g + 1], (ID_ROWS // 2, lanes)),
                jnp.broadcast_to(low[g : g + 1], (ID_ROWS // 2, lanes)),
            ],
            axis=0,
        )
        ids = ids + dot(pair, part, ((1,), (1,)))
    ids = ids.astype(BF16)
    moved = dot(pick_ref[...], emb_ref[...]).astype(BF16)
    width = emb_ref.shape[1]
    for j in range(n_seq):
        send_ref[j, :cap] = moved[j * cap : (j + 1) * cap]
        digits = ids[:, j * cap : (j + 1) * cap]
        rest = jnp.zeros((ID_ROWS, width - cap), BF16)
        send_ref[j, cap:] = jnp.concatenate([digits, rest], axis=1)


def pack_kernel(n_seq, cap, start, widths, pick_ref, emb_ref, *send_refs):
    first = start
    for send_ref, width in zip(send_refs, widths):
        moved = dot(pick_ref[...], emb_ref[:, first : first + width]).astype(BF16)
        for j in range(n_seq):
            send_ref[j] = moved[j * cap : (j + 1) * cap]
        first += width


def hidden_kernel(height, me_ref, pre_ref, mine_ref, theirs_ref, slope_ref):
    values = pre_ref[...].astype(F32)
    normal_cdf = 0.5 * (1.0 + lax.erf(values * (1.0 / math.sqrt(2.0))))
    density = jnp.exp(-0.5 * values * values) * (1.0 / math.sqrt(2.0 * math.pi))
    slope_ref[...] = normal_cdf + values * density
    hidden = (values * normal_cdf).astype(BF16).T
    even_mine = lax.bitwise_and(me_ref[1], 1) == 0
    for k in range(mine_ref.shape[0] // height):
        even = hidden[2 * k * height : (2 * k + 1) * height]
        odd = hidden[(2 * k + 1) * height : (2 * k + 2) * height]
        mine_ref[k * height : (k + 1) * height] = jnp.where(even_mine, even, odd)
        theirs_ref[k * height : (k + 1) * height] = jnp.where(even_mine, odd, even)


def landing_kernel(n_seq, cap, rows_dev, got_ref, land_ref):
    lows = ID_ROWS // 2
    ids = []
    for i in range(n_seq):
        digits = got_ref[i, cap:].astype(F32)[:, :cap]
        ids.append(digits[0:1] * float(ID_BASE) + digits[lows : lows + 1])
    ids = jnp.concatenate(ids, axis=1).astype(I32) - 1
    slots = ids.shape[1]
    step = 128
    for first in range(0, rows_dev, step):
        row = lax.broadcasted_iota(I32, (step, slots), 0) + first
        land_ref[first : first + step] = (row == ids).astype(F32).astype(BF16)


def place_kernel(n_seq, cap, land_ref, got_ref, placed_ref):
    got = jnp.concatenate([got_ref[i, :cap] for i in range(n_seq)], axis=0)
    placed_ref[...] = dot(land_ref[...], got).astype(BF16)


def share_kernel(n_seq, n_pairs, height, me_ref, mine_ref, theirs_ref, own_ref, other_ref, *refs):
    away_a, keep_a, away_b, keep_b = refs
    step = pl.program_id(0)
    share = dot(mine_ref[...], own_ref[...]) + dot(theirs_ref[...], other_ref[...])
    width = share.shape[1] // 2
    n_far = n_seq // 2
    my_low = lax.bitwise_and(me_ref[0], 1)
    my_pair = lax.shift_right_logical(me_ref[1], 1)
    per_step = mine_ref.shape[0] // (height * n_pairs)
    half = n_pairs // 2

    def block(a, p, column):
        first = (a * n_pairs + p) * height
        return share[first : first + height, column : column + width]

    for a in range(per_step):
        far = (step * per_step + a) // 2
        for p in range(half):
            low, high = block(a, p, 0), block(a, p + half, 0)
            low_mine = my_pair < half
            at = lax.bitwise_xor(p, lax.bitwise_and(my_pair, half - 1)) * n_seq
            at = at + lax.bitwise_xor(a % 2, my_low) * n_far + far
            keep_a[at] = jnp.where(low_mine, low, high)
            away_a[at] = jnp.where(low_mine, high, low).astype(BF16)
    for a in range(0, per_step, 2):
        far = (step * per_step + a) // 2
        for p in range(n_pairs):
            low, high = block(a, p, width), block(a + 1, p, width)
            at = lax.bitwise_xor(p, my_pair) * n_far + far
            keep_b[at] = jnp.where(my_low == 0, low, high)
            away_b[at] = jnp.where(my_low == 0, high, low).astype(BF16)


def add_kernel(keep_a, come_a, keep_b, come_b, send_a, stay_a, send_b, stay_b):
    for keep, come, send, stay in ((keep_a, come_a, send_a, stay_a), (keep_b, come_b, send_b, stay_b)):
        n = stay.shape[0]
        stay[...] = keep[:n] + come[:n].astype(F32)
        send[...] = (keep[n:] + come[n:].astype(F32)).astype(BF16)


def add_join_kernel(keep_a, come_a, keep_b, come_b, out_ref):
    half = keep_a.shape[2]
    out_ref[:, :, :half] = (keep_a[...] + come_a[...].astype(F32)).astype(BF16)
    out_ref[:, :, half:] = (keep_b[...] + come_b[...].astype(F32)).astype(BF16)


def total_kernel(normalizer, come_ref, out_ref):
    total = come_ref[0].astype(F32)
    for k in range(1, come_ref.shape[0]):
        total = total + come_ref[k].astype(F32)
    out_ref[0] = total * normalizer


def weight_kernel(n_pieces, me_ref, *refs):
    refs, out_refs = refs[: 4 * n_pieces], refs[4 * n_pieces :]
    even_mine = lax.bitwise_and(me_ref[1], 1) == 0
    start = 0
    for k in range(2):
        mine_refs, their_refs, refs = refs[:n_pieces], refs[n_pieces : 2 * n_pieces], refs[2 * n_pieces :]
        blocks = []
        for mine, theirs in zip(mine_refs, their_refs):
            blocks.append(jnp.where(even_mine, mine[0], theirs[0]))
            blocks.append(jnp.where(even_mine, theirs[0], mine[0]))
        columns = jnp.concatenate(blocks, axis=0).T
        stop = start + columns.shape[0]
        first = 0
        for out_ref in out_refs:
            low, high = max(start, first), min(stop, first + out_ref.shape[0])
            if low < high:
                out_ref[low - first : high - first] = columns[low - start : high - start]
            first += out_ref.shape[0]
        start = stop


def act_kernel(n_parts, *refs):
    placed_refs, weight_refs, refs = refs[:n_parts], refs[n_parts : 2 * n_parts], refs[2 * n_parts :]
    slope_ref, out_ref = refs
    grad = dot(placed_refs[0][...], weight_refs[0][...])
    for placed_ref, weight_ref in zip(placed_refs[1:], weight_refs[1:]):
        grad = grad + dot(placed_ref[...], weight_ref[...])
    out_ref[...] = (grad * slope_ref[...]).astype(BF16)


def join_kernel(n_dp, me_ref, *refs):
    out_ref = refs[-1]
    height = out_ref.shape[0] // n_dp
    for q in range(n_dp):
        v = lax.bitwise_xor(me_ref[1], q)
        value = refs[0][0]
        for r in range(1, n_dp):
            value = jnp.where(v == r, refs[r][0], value)
        out_ref[q * height : (q + 1) * height] = value


def swap(value, axis, bit):
    size = lax.axis_size(axis)
    return lax.ppermute(value, axis, [(i, i ^ (1 << bit)) for i in range(size)])


def local(emb_grad, image_map, pre_act, w_down):
    n_seq, n_dp = lax.axis_size("seq"), lax.axis_size("dp")
    seq_bits, dp_bits = n_seq.bit_length() - 1, n_dp.bit_length() - 1
    me_s = lax.axis_index("seq").astype(I32)
    me_d = lax.axis_index("dp").astype(I32)
    me = jnp.stack([me_s, me_d])
    tokens, dim = emb_grad.shape[1:]
    rows_dev, hid = pre_act.shape[1:]
    cap = rows_dev // n_seq
    slots = n_seq * cap
    emb, pre = emb_grad[0], pre_act[0]
    n_parts = len(WIDTHS)
    last = n_parts - 1
    height = hid // (n_seq * n_dp)
    n_pairs = n_dp // 2
    kept = n_seq * n_pairs // 2
    normalizer = 1.0 / math.sqrt(n_dp * rows_dev * n_seq)
    smem = pl.BlockSpec(memory_space=pltpu.SMEM)
    anywhere = pl.BlockSpec(memory_space=pl.ANY)
    shape = jax.ShapeDtypeStruct
    cheap = cost(1e6, 1e5)
    clock = None
    flying = {}

    def call(body, operands, in_specs, outs, mib, name, grid=(1,), scratch=(), aliases=None):
        nonlocal clock
        given = [] if clock is None else [clock]

        def timed(*refs):
            n_in = len(operands)
            ins, refs = refs[:n_in], refs[n_in + len(given) :]
            refs[len(outs)][...] = jnp.zeros((8, 128), F32)
            body(*ins, *refs[: len(outs)], *refs[len(outs) + 1 :])

        *results, clock = pl.pallas_call(
            timed,
            grid=grid,
            in_specs=list(in_specs) + [anywhere] * len(given),
            out_specs=[block for _, block in outs] + [whole(8, 128)],
            out_shape=[one for one, _ in outs] + [shape((8, 128), F32)],
            scratch_shapes=list(scratch),
            input_output_aliases=aliases or {},
            compiler_params=params(mib),
            cost_estimate=cheap,
            name=name,
        )(*operands, *given)
        return results

    def order(*values):
        nonlocal clock
        *values, clock = lax.optimization_barrier((*values, clock))
        return values

    def boundary(*beyond):
        names = [n for n in flying if n not in beyond]
        values = order(*[flying.pop(n) for n in names])
        return dict(zip(names, values))

    def exchange(blocks):
        return lax.all_to_all(blocks, "seq", split_axis=0, concat_axis=0, tiled=True)

    w_near = [lax.dynamic_slice(w_down, (me_d * height, 0), (height, dim))[None]]
    w_bits = [("seq", bit) for bit in reversed(range(1, seq_bits))]
    far = [("dp", bit) for bit in reversed(range(1, dp_bits))]
    w_orders = [w_bits + [("seq", 0)] + far, w_bits + far + [("seq", 0)]]
    w_done = [0]
    w_names = (("w", 0), ("w", 1))

    def more_weights():
        at = w_done[0]
        if at:
            for k in range(len(w_near)):
                come = landed["w", k]
                bit = lax.bitwise_and(
                    lax.shift_right_logical(me_s if w_orders[k][at - 1][0] == "seq" else me_d, w_orders[k][at - 1][1]), 1
                )
                halves = jnp.where(bit == 0, w_near[k], come), jnp.where(bit == 0, come, w_near[k])
                w_near[k] = jnp.concatenate(halves, axis=0)
        if at == len(w_bits):
            w_near[:] = [w_near[0][:, :, : dim // 2], w_near[0][:, :, dim // 2 :]]
        for k in range(len(w_near)):
            flying["w", k] = swap(w_near[k], *(w_orders[k][at] if at < len(w_orders[k]) else ("dp", 0)))
        w_done[0] += 1

    more_weights()

    pick, sends = call(
        functools.partial(route_kernel, n_seq, cap, rows_dev),
        [image_map.reshape(tokens // 128, 128), emb],
        [whole(tokens // 128, 128), whole(tokens, WIDTHS[0])],
        [
            (shape((slots, tokens), BF16), whole(slots, tokens)),
            (
                shape((n_seq, cap + ID_ROWS, WIDTHS[0]), BF16),
                whole(n_seq, cap + ID_ROWS, WIDTHS[0]),
            ),
        ],
        60,
        "route",
    )
    rest = WIDTHS[1:]
    packed = call(
        functools.partial(pack_kernel, n_seq, cap, WIDTHS[0], rest),
        [pick, emb],
        [whole(slots, tokens), whole(tokens, dim)],
        [(shape((n_seq, cap, w), BF16), whole(n_seq, cap, w)) for w in rest],
        60,
        "pack",
    )
    landed = boundary()
    [sends] = order(sends)
    flying["got"] = exchange(sends)
    more_weights()
    mine_t, away_t, slope = call(
        functools.partial(hidden_kernel, height),
        [me, pre],
        [smem, pl.BlockSpec((rows_dev, GROUP), lambda i: (0, i))],
        [(shape((hid // 2, rows_dev), BF16), pl.BlockSpec((GROUP // 2, rows_dev), lambda i: (i, 0)))] * 2
        + [(shape((rows_dev, hid), F32), pl.BlockSpec((rows_dev, GROUP), lambda i: (0, i)))],
        60,
        "hidden",
        grid=(hid // GROUP,),
    )
    flying["hidden"] = swap(away_t, "dp", 0)

    far = [("dp", bit) for bit in reversed(range(1, dp_bits))]
    paths = (far + [("seq", 0)], [("seq", 0)] + far)
    columns = [[low + 2 * k for k in range(n_seq // 2)] for low in range(2)]
    placed_parts, sums, done, grads = [], [], [], {}

    def place(c):
        got = landed["got"]
        [placed] = call(
            functools.partial(place_kernel, n_seq, cap),
            [land, got],
            [whole(rows_dev, slots), whole(*got.shape)],
            [(shape((rows_dev, WIDTHS[c]), BF16), whole(rows_dev, WIDTHS[c]))],
            16,
            "place",
        )
        placed_parts.append(placed)
        return swap(placed, "dp", 0)

    def share(c, other):
        width = WIDTHS[c]
        half = width // 2
        *halves, = call(
            functools.partial(share_kernel, n_seq, n_pairs, height),
            [me, mine_t, theirs_t, placed_parts[c], other],
            [smem]
            + [pl.BlockSpec((GROUP // 2, rows_dev), lambda i: (i, 0))] * 2
            + [whole(rows_dev, width)] * 2,
            [(shape((kept, height, half), t), whole(kept, height, half)) for t in (BF16, F32, BF16, F32)],
            40,
            "share",
            grid=(hid // GROUP,),
        )
        sums.append([halves[1], halves[3]])
        done.append(1)
        for k in range(2):
            flying["sum", c, k] = swap(halves[2 * k], *paths[k][0])

    def advance():
        for c in reversed(range(len(sums))):
            names = [name for name in landed if name[0] == "sum" and name[1] == c]
            if not names:
                continue
            come = [landed[name] for name in names]
            at = done[c]
            done[c] += 1
            width = WIDTHS[c]
            if at > len(paths[0]):
                [grads[c]] = call(
                    functools.partial(total_kernel, normalizer),
                    come,
                    [whole(*come[0].shape)],
                    [(shape((1, height, width), F32), whole(1, height, width))],
                    24,
                    "total",
                )
                continue
            terms = [sums[c][0], come[0], sums[c][1], come[1]]
            specs = [whole(*one.shape) for one in terms]
            n = terms[0].shape[0]
            if at < len(paths[0]):
                sizes = (n // 2, height, width // 2)
                results = call(
                    add_kernel,
                    terms,
                    specs,
                    [(shape(sizes, t), whole(*sizes)) for t in (BF16, F32, BF16, F32)],
                    40,
                    "add",
                )
                sums[c] = [results[1], results[3]]
                for k in range(2):
                    flying["sum", c, k] = swap(results[2 * k], *paths[k][at])
            else:
                [sent] = call(
                    add_join_kernel,
                    terms,
                    specs,
                    [(shape((n, height, width), BF16), whole(n, height, width))],
                    40,
                    "add_join",
                )
                flying["sum", c, 0] = lax.all_to_all(
                    sent, "seq", split_axis=0, concat_axis=0, tiled=True, axis_index_groups=columns
                )

    spreads = {}

    def spread():
        for c in range(n_parts):
            if ("spread", c) in landed:
                found, bit = spreads[c]
                come = landed["spread", c]
                for at, v in enumerate(list(found)):
                    found[v + (1 << bit)] = come[at : at + 1]
            elif c not in spreads and c in grads:
                found, bit = {0: grads[c]}, dp_bits
            else:
                continue
            spreads[c] = (found, bit - 1)
            if bit:
                sent = jnp.concatenate(list(found.values()), axis=0) if len(found) > 1 else found[0]
                flying["spread", c] = swap(sent, "dp", bit - 1)

    def join(pieces, column, base):
        width = pieces[0].shape[2]
        block = math.gcd(column, width)
        more = [] if base is None else [base]
        return call(
            lambda *refs: join_kernel(n_dp, *refs[: n_dp + 1], refs[-1]),
            [me, *pieces, *more],
            [smem] + [pl.BlockSpec((1, height, block), lambda i: (0, 0, i))] * n_dp + [anywhere] * len(more),
            [
                (
                    shape((n_dp * height, dim), F32),
                    pl.BlockSpec((n_dp * height, block), lambda i: (0, i + column // block)),
                )
            ],
            24,
            "join",
            grid=(width // block,),
            aliases={n_dp + 1: 0} if more else {},
        )[0]

    def finish_weights(landed):
        n_pieces = GROUP // (2 * height)

        def spec(half, k):
            def index(i):
                flat = i * n_pieces + k
                s, d_high = lax.div(flat, n_pairs), lax.rem(flat, n_pairs)
                place = 0
                for at, (axis, bit) in enumerate(w_orders[half]):
                    one = lax.shift_right_logical(s, bit) if axis == "seq" else lax.shift_right_logical(d_high, bit - 1)
                    place = place + lax.bitwise_and(one, 1) * (1 << at)
                return (place, 0, 0)

            return pl.BlockSpec((1, height, dim // 2), index)

        return call(
            functools.partial(weight_kernel, n_pieces),
            [me, *[one for k in range(2) for part in (w_near[k], landed["w", k]) for one in [part] * n_pieces]],
            [smem] + [spec(half, k) for half in range(2) for _ in range(2) for k in range(n_pieces)],
            [(shape((w, hid), BF16), pl.BlockSpec((w, GROUP), lambda i: (0, i))) for w in WIDTHS],
            40,
            "weights",
            grid=(hid // GROUP,),
        )

    def act(first, blocks, base):
        block = 256
        tile = pl.BlockSpec((rows_dev, block), lambda i: (0, i + first))
        more = [] if base is None else [base]
        n_in = 2 * n_parts + 1
        return call(
            lambda *refs: act_kernel(n_parts, *refs[:n_in], refs[-1]),
            [*placed_parts, *weights_t, slope, *more],
            [whole(rows_dev, w) for w in WIDTHS]
            + [pl.BlockSpec((w, block), lambda i: (0, i + first)) for w in WIDTHS]
            + [tile]
            + [anywhere] * len(more),
            [(shape((rows_dev, hid), BF16), tile)],
            60,
            "act",
            grid=(blocks,),
            aliases={n_in: 0} if more else {},
        )[0]

    for _ in range(len(w_bits) - 2):
        landed = boundary("got", "hidden")
        more_weights()
    landed = boundary()
    theirs_t = landed["hidden"]
    [land] = call(
        functools.partial(landing_kernel, n_seq, cap, rows_dev),
        [landed["got"]],
        [whole(n_seq, cap + ID_ROWS, WIDTHS[0])],
        [(shape((rows_dev, slots), BF16), whole(rows_dev, slots))],
        16,
        "landing",
    )
    act_grad = None
    cuts = [(0, 6), (6, 4)]
    assert n_parts == 2
    for c in range(n_parts):
        if c < last:
            flying["got"] = exchange(packed[c])
        if w_names[0] in landed:
            more_weights()
        share(c, place(c))
        advance()
        landed = boundary()
    w_grad = None
    joined = 0
    while joined < n_parts:
        advance()
        spread()
        if w_names[0] in landed:
            more_weights()
            w_last = boundary(*[name for name in flying if name not in w_names])
            weights_t = finish_weights(w_last)
            act_grad = act(*cuts.pop(0), None)
        elif cuts:
            act_grad = act(*cuts.pop(0), act_grad)
        while joined < n_parts and joined in spreads and len(spreads[joined][0]) == n_dp:
            found = spreads[joined][0]
            w_grad = join([found[v] for v in range(n_dp)], sum(WIDTHS[:joined]), w_grad)
            joined += 1
        if flying:
            landed = boundary()
    return act_grad[None], w_grad


def solution(mesh):
    placed = (P("dp", "seq", None), P("dp", "seq"), P("dp", "seq", None), P("seq", None))
    return jax.shard_map(
        local,
        mesh=mesh,
        in_specs=placed,
        out_specs=(P("dp", "seq", None), P("seq", None)),
        check_vma=False,
    )
```

```python
import functools
import math

import jax
import jax.numpy as jnp
from jax import lax
from jax.experimental import pallas as pl
from jax.experimental.pallas import tpu as pltpu
from jax.sharding import PartitionSpec as P

F32, BF16, I32 = jnp.float32, jnp.bfloat16, jnp.int32
MIB = 2**20
WIDTHS = (1024, 768)
ID_BASE = 32
ID_ROWS = 16
GROUP = 640


def dot(a, b, dims=((1,), (0,))):
    return lax.dot_general(a, b, (dims, ((), ())), preferred_element_type=F32)


def params(mib):
    return pltpu.CompilerParams(vmem_limit_bytes=mib * MIB)


def cost(flops, nbytes):
    return pl.CostEstimate(flops=int(flops), bytes_accessed=int(nbytes), transcendentals=0)


def whole(*dims):
    return pl.BlockSpec(dims, lambda *_: (0,) * len(dims))


def reverse(index, bits):
    back = 0
    for bit in range(bits):
        one = lax.bitwise_and(lax.shift_right_logical(index, bit), 1)
        back = back + one * (1 << (bits - 1 - bit))
    return back


def route_kernel(n_seq, cap, rows_dev, map_ref, emb_ref, pick_ref, send_ref):
    targets = map_ref[...]
    groups, lanes = targets.shape
    live = targets >= 0
    safe = jnp.where(live, targets, 0)
    owner = jnp.where(live, lax.div(safe, rows_dev), n_seq)
    members = [(owner == j).astype(F32) for j in range(n_seq)]
    table = jnp.concatenate(members, axis=0).astype(BF16)
    upper = (
        lax.broadcasted_iota(I32, (lanes, lanes), 0) < lax.broadcasted_iota(I32, (lanes, lanes), 1)
    ).astype(F32).astype(BF16)
    inside = dot(table, upper)
    total = n_seq * groups
    row = lax.broadcasted_iota(I32, (total, total), 0)
    col = lax.broadcasted_iota(I32, (total, total), 1)
    earlier = ((lax.div(row, groups) == lax.div(col, groups)) & (col < row)).astype(F32).astype(BF16)
    counts = dot(table, jnp.ones((lanes, lanes), BF16))
    rank_all = inside + dot(earlier, counts.astype(BF16))
    rank = jnp.zeros((groups, lanes), F32)
    for j in range(n_seq):
        rank = rank + members[j] * rank_all[j * groups : (j + 1) * groups]
    slot = jnp.where(live, owner * cap + rank.astype(I32), -1)
    number = jnp.where(live, safe - owner * rows_dev + 1, 0)
    high = lax.div(number, ID_BASE)
    low = (number - high * ID_BASE).astype(F32).astype(BF16)
    high = high.astype(F32).astype(BF16)
    slots = n_seq * cap
    place = lax.broadcasted_iota(I32, (slots, lanes), 0)
    ids = jnp.zeros((ID_ROWS, slots), F32)
    for g in range(groups):
        part = (place == slot[g : g + 1]).astype(F32).astype(BF16)
        pick_ref[:, g * lanes : (g + 1) * lanes] = part
        pair = jnp.concatenate(
            [
                jnp.broadcast_to(high[g : g + 1], (ID_ROWS // 2, lanes)),
                jnp.broadcast_to(low[g : g + 1], (ID_ROWS // 2, lanes)),
            ],
            axis=0,
        )
        ids = ids + dot(pair, part, ((1,), (1,)))
    ids = ids.astype(BF16)
    moved = dot(pick_ref[...], emb_ref[...]).astype(BF16)
    width = emb_ref.shape[1]
    for j in range(n_seq):
        send_ref[j, :cap] = moved[j * cap : (j + 1) * cap]
        digits = ids[:, j * cap : (j + 1) * cap]
        rest = jnp.zeros((ID_ROWS, width - cap), BF16)
        send_ref[j, cap:] = jnp.concatenate([digits, rest], axis=1)


def pack_kernel(n_seq, cap, start, widths, pick_ref, emb_ref, *send_refs):
    first = start
    for send_ref, width in zip(send_refs, widths):
        moved = dot(pick_ref[...], emb_ref[:, first : first + width]).astype(BF16)
        for j in range(n_seq):
            send_ref[j] = moved[j * cap : (j + 1) * cap]
        first += width


def hidden_kernel(height, me_ref, pre_ref, mine_ref, theirs_ref, slope_ref):
    values = pre_ref[...].astype(F32)
    normal_cdf = 0.5 * (1.0 + lax.erf(values * (1.0 / math.sqrt(2.0))))
    density = jnp.exp(-0.5 * values * values) * (1.0 / math.sqrt(2.0 * math.pi))
    slope_ref[...] = normal_cdf + values * density
    hidden = (values * normal_cdf).astype(BF16).T
    even_mine = lax.bitwise_and(me_ref[1], 1) == 0
    for k in range(mine_ref.shape[0] // height):
        even = hidden[2 * k * height : (2 * k + 1) * height]
        odd = hidden[(2 * k + 1) * height : (2 * k + 2) * height]
        mine_ref[k * height : (k + 1) * height] = jnp.where(even_mine, even, odd)
        theirs_ref[k * height : (k + 1) * height] = jnp.where(even_mine, odd, even)


def landing_kernel(n_seq, cap, rows_dev, got_ref, land_ref):
    lows = ID_ROWS // 2
    ids = []
    for i in range(n_seq):
        digits = got_ref[i, cap:].astype(F32)[:, :cap]
        ids.append(digits[0:1] * float(ID_BASE) + digits[lows : lows + 1])
    ids = jnp.concatenate(ids, axis=1).astype(I32) - 1
    slots = ids.shape[1]
    step = 128
    for first in range(0, rows_dev, step):
        row = lax.broadcasted_iota(I32, (step, slots), 0) + first
        land_ref[first : first + step] = (row == ids).astype(F32).astype(BF16)


def place_kernel(n_seq, cap, land_ref, got_ref, placed_ref):
    got = jnp.concatenate([got_ref[i, :cap] for i in range(n_seq)], axis=0)
    placed_ref[...] = dot(land_ref[...], got).astype(BF16)


def share_kernel(n_seq, n_pairs, height, me_ref, mine_ref, theirs_ref, own_ref, other_ref, *refs):
    away_a, keep_a, away_b, keep_b = refs
    step = pl.program_id(0)
    share = dot(mine_ref[...], own_ref[...]) + dot(theirs_ref[...], other_ref[...])
    width = share.shape[1] // 2
    n_far = n_seq // 2
    my_low = lax.bitwise_and(me_ref[0], 1)
    my_pair = lax.shift_right_logical(me_ref[1], 1)
    per_step = mine_ref.shape[0] // (height * n_pairs)
    half = n_pairs // 2

    def block(a, p, column):
        first = (a * n_pairs + p) * height
        return share[first : first + height, column : column + width]

    for a in range(per_step):
        far = (step * per_step + a) // 2
        for p in range(half):
            low, high = block(a, p, 0), block(a, p + half, 0)
            low_mine = my_pair < half
            at = lax.bitwise_xor(p, lax.bitwise_and(my_pair, half - 1)) * n_seq
            at = at + lax.bitwise_xor(a % 2, my_low) * n_far + far
            keep_a[at] = jnp.where(low_mine, low, high)
            away_a[at] = jnp.where(low_mine, high, low).astype(BF16)
    for a in range(0, per_step, 2):
        far = (step * per_step + a) // 2
        for p in range(n_pairs):
            low, high = block(a, p, width), block(a + 1, p, width)
            at = lax.bitwise_xor(p, my_pair) * n_far + far
            keep_b[at] = jnp.where(my_low == 0, low, high)
            away_b[at] = jnp.where(my_low == 0, high, low).astype(BF16)


def add_kernel(keep_a, come_a, keep_b, come_b, send_a, stay_a, send_b, stay_b):
    for keep, come, send, stay in ((keep_a, come_a, send_a, stay_a), (keep_b, come_b, send_b, stay_b)):
        n = stay.shape[0]
        stay[...] = keep[:n] + come[:n].astype(F32)
        send[...] = (keep[n:] + come[n:].astype(F32)).astype(BF16)


def add_join_kernel(keep_a, come_a, keep_b, come_b, out_ref):
    half = keep_a.shape[2]
    out_ref[:, :, :half] = (keep_a[...] + come_a[...].astype(F32)).astype(BF16)
    out_ref[:, :, half:] = (keep_b[...] + come_b[...].astype(F32)).astype(BF16)


def total_kernel(normalizer, come_ref, out_ref):
    total = come_ref[0].astype(F32)
    for k in range(1, come_ref.shape[0]):
        total = total + come_ref[k].astype(F32)
    out_ref[0] = total * normalizer


def weight_kernel(n_pieces, me_ref, *refs):
    refs, out_refs = refs[: 4 * n_pieces], refs[4 * n_pieces :]
    even_mine = lax.bitwise_and(me_ref[1], 1) == 0
    start = 0
    for k in range(2):
        mine_refs, their_refs, refs = refs[:n_pieces], refs[n_pieces : 2 * n_pieces], refs[2 * n_pieces :]
        blocks = []
        for mine, theirs in zip(mine_refs, their_refs):
            blocks.append(jnp.where(even_mine, mine[0], theirs[0]))
            blocks.append(jnp.where(even_mine, theirs[0], mine[0]))
        columns = jnp.concatenate(blocks, axis=0).T
        stop = start + columns.shape[0]
        first = 0
        for out_ref in out_refs:
            low, high = max(start, first), min(stop, first + out_ref.shape[0])
            if low < high:
                out_ref[low - first : high - first] = columns[low - start : high - start]
            first += out_ref.shape[0]
        start = stop


def act_kernel(n_parts, *refs):
    placed_refs, weight_refs, refs = refs[:n_parts], refs[n_parts : 2 * n_parts], refs[2 * n_parts :]
    slope_ref, out_ref = refs
    grad = dot(placed_refs[0][...], weight_refs[0][...])
    for placed_ref, weight_ref in zip(placed_refs[1:], weight_refs[1:]):
        grad = grad + dot(placed_ref[...], weight_ref[...])
    out_ref[...] = (grad * slope_ref[...]).astype(BF16)


def join_kernel(n_dp, me_ref, *refs):
    out_ref = refs[-1]
    height = out_ref.shape[0] // n_dp
    for q in range(n_dp):
        v = lax.bitwise_xor(me_ref[1], q)
        value = refs[0][0]
        for r in range(1, n_dp):
            value = jnp.where(v == r, refs[r][0], value)
        out_ref[q * height : (q + 1) * height] = value


def swap(value, axis, bit):
    size = lax.axis_size(axis)
    return lax.ppermute(value, axis, [(i, i ^ (1 << bit)) for i in range(size)])


def local(emb_grad, image_map, pre_act, w_down):
    n_seq, n_dp = lax.axis_size("seq"), lax.axis_size("dp")
    seq_bits, dp_bits = n_seq.bit_length() - 1, n_dp.bit_length() - 1
    me_s = lax.axis_index("seq").astype(I32)
    me_d = lax.axis_index("dp").astype(I32)
    me = jnp.stack([me_s, me_d])
    tokens, dim = emb_grad.shape[1:]
    rows_dev, hid = pre_act.shape[1:]
    cap = rows_dev // n_seq
    slots = n_seq * cap
    emb, pre = emb_grad[0], pre_act[0]
    n_parts = len(WIDTHS)
    last = n_parts - 1
    height = hid // (n_seq * n_dp)
    n_pairs = n_dp // 2
    kept = n_seq * n_pairs // 2
    normalizer = 1.0 / math.sqrt(n_dp * rows_dev * n_seq)
    smem = pl.BlockSpec(memory_space=pltpu.SMEM)
    anywhere = pl.BlockSpec(memory_space=pl.ANY)
    shape = jax.ShapeDtypeStruct
    cheap = cost(1e6, 1e5)
    clock = None
    flying = {}

    def call(body, operands, in_specs, outs, mib, name, grid=(1,), scratch=(), aliases=None):
        nonlocal clock
        given = [] if clock is None else [clock]

        def timed(*refs):
            n_in = len(operands)
            ins, refs = refs[:n_in], refs[n_in + len(given) :]
            refs[len(outs)][...] = jnp.zeros((8, 128), F32)
            body(*ins, *refs[: len(outs)], *refs[len(outs) + 1 :])

        *results, clock = pl.pallas_call(
            timed,
            grid=grid,
            in_specs=list(in_specs) + [anywhere] * len(given),
            out_specs=[block for _, block in outs] + [whole(8, 128)],
            out_shape=[one for one, _ in outs] + [shape((8, 128), F32)],
            scratch_shapes=list(scratch),
            input_output_aliases=aliases or {},
            compiler_params=params(mib),
            cost_estimate=cheap,
            name=name,
        )(*operands, *given)
        return results

    def order(*values):
        nonlocal clock
        *values, clock = lax.optimization_barrier((*values, clock))
        return values

    def boundary(*beyond):
        names = [n for n in flying if n not in beyond]
        values = order(*[flying.pop(n) for n in names])
        return dict(zip(names, values))

    def exchange(blocks):
        return lax.all_to_all(blocks, "seq", split_axis=0, concat_axis=0, tiled=True)

    w_near = [lax.dynamic_slice(w_down, (me_d * height, 0), (height, dim))[None]]
    w_bits = [("seq", bit) for bit in reversed(range(1, seq_bits))]
    far = [("dp", bit) for bit in reversed(range(1, dp_bits))]
    w_orders = [w_bits + [("seq", 0)] + far, w_bits + far + [("seq", 0)]]
    w_done = [0]
    w_names = (("w", 0), ("w", 1))

    def more_weights():
        at = w_done[0]
        if at:
            for k in range(len(w_near)):
                come = landed["w", k]
                bit = lax.bitwise_and(
                    lax.shift_right_logical(me_s if w_orders[k][at - 1][0] == "seq" else me_d, w_orders[k][at - 1][1]), 1
                )
                halves = jnp.where(bit == 0, w_near[k], come), jnp.where(bit == 0, come, w_near[k])
                w_near[k] = jnp.concatenate(halves, axis=0)
        if at == len(w_bits):
            w_near[:] = [w_near[0][:, :, : dim // 2], w_near[0][:, :, dim // 2 :]]
        for k in range(len(w_near)):
            flying["w", k] = swap(w_near[k], *(w_orders[k][at] if at < len(w_orders[k]) else ("dp", 0)))
        w_done[0] += 1

    more_weights()

    pick, sends = call(
        functools.partial(route_kernel, n_seq, cap, rows_dev),
        [image_map.reshape(tokens // 128, 128), emb],
        [whole(tokens // 128, 128), whole(tokens, WIDTHS[0])],
        [
            (shape((slots, tokens), BF16), whole(slots, tokens)),
            (
                shape((n_seq, cap + ID_ROWS, WIDTHS[0]), BF16),
                whole(n_seq, cap + ID_ROWS, WIDTHS[0]),
            ),
        ],
        60,
        "route",
    )
    rest = WIDTHS[1:]
    packed = call(
        functools.partial(pack_kernel, n_seq, cap, WIDTHS[0], rest),
        [pick, emb],
        [whole(slots, tokens), whole(tokens, dim)],
        [(shape((n_seq, cap, w), BF16), whole(n_seq, cap, w)) for w in rest],
        60,
        "pack",
    )
    landed = boundary()
    [sends] = order(sends)
    flying["got"] = exchange(sends)
    more_weights()
    mine_t, away_t, slope = call(
        functools.partial(hidden_kernel, height),
        [me, pre],
        [smem, pl.BlockSpec((rows_dev, GROUP), lambda i: (0, i))],
        [(shape((hid // 2, rows_dev), BF16), pl.BlockSpec((GROUP // 2, rows_dev), lambda i: (i, 0)))] * 2
        + [(shape((rows_dev, hid), F32), pl.BlockSpec((rows_dev, GROUP), lambda i: (0, i)))],
        60,
        "hidden",
        grid=(hid // GROUP,),
    )
    flying["hidden"] = swap(away_t, "dp", 0)

    far = [("dp", bit) for bit in reversed(range(1, dp_bits))]
    paths = (far + [("seq", 0)], [("seq", 0)] + far)
    columns = [[low + 2 * k for k in range(n_seq // 2)] for low in range(2)]
    placed_parts, sums, done, grads = [], [], [], {}

    def place(c):
        got = landed["got"]
        [placed] = call(
            functools.partial(place_kernel, n_seq, cap),
            [land, got],
            [whole(rows_dev, slots), whole(*got.shape)],
            [(shape((rows_dev, WIDTHS[c]), BF16), whole(rows_dev, WIDTHS[c]))],
            16,
            "place",
        )
        placed_parts.append(placed)
        return swap(placed, "dp", 0)

    def share(c, other):
        width = WIDTHS[c]
        half = width // 2
        *halves, = call(
            functools.partial(share_kernel, n_seq, n_pairs, height),
            [me, mine_t, theirs_t, placed_parts[c], other],
            [smem]
            + [pl.BlockSpec((GROUP // 2, rows_dev), lambda i: (i, 0))] * 2
            + [whole(rows_dev, width)] * 2,
            [(shape((kept, height, half), t), whole(kept, height, half)) for t in (BF16, F32, BF16, F32)],
            40,
            "share",
            grid=(hid // GROUP,),
        )
        sums.append([halves[1], halves[3]])
        done.append(1)
        for k in range(2):
            flying["sum", c, k] = swap(halves[2 * k], *paths[k][0])

    def advance():
        for c in reversed(range(len(sums))):
            names = [name for name in landed if name[0] == "sum" and name[1] == c]
            if not names:
                continue
            come = [landed[name] for name in names]
            at = done[c]
            done[c] += 1
            width = WIDTHS[c]
            if at > len(paths[0]):
                [grads[c]] = call(
                    functools.partial(total_kernel, normalizer),
                    come,
                    [whole(*come[0].shape)],
                    [(shape((1, height, width), F32), whole(1, height, width))],
                    24,
                    "total",
                )
                continue
            terms = [sums[c][0], come[0], sums[c][1], come[1]]
            specs = [whole(*one.shape) for one in terms]
            n = terms[0].shape[0]
            if at < len(paths[0]):
                sizes = (n // 2, height, width // 2)
                results = call(
                    add_kernel,
                    terms,
                    specs,
                    [(shape(sizes, t), whole(*sizes)) for t in (BF16, F32, BF16, F32)],
                    40,
                    "add",
                )
                sums[c] = [results[1], results[3]]
                for k in range(2):
                    flying["sum", c, k] = swap(results[2 * k], *paths[k][at])
            else:
                [sent] = call(
                    add_join_kernel,
                    terms,
                    specs,
                    [(shape((n, height, width), BF16), whole(n, height, width))],
                    40,
                    "add_join",
                )
                flying["sum", c, 0] = lax.all_to_all(
                    sent, "seq", split_axis=0, concat_axis=0, tiled=True, axis_index_groups=columns
                )

    spreads = {}

    def spread():
        for c in range(n_parts):
            if ("spread", c) in landed:
                found, bit = spreads[c]
                come = landed["spread", c]
                for at, v in enumerate(list(found)):
                    found[v + (1 << bit)] = come[at : at + 1]
            elif c not in spreads and c in grads:
                found, bit = {0: grads[c]}, dp_bits
            else:
                continue
            spreads[c] = (found, bit - 1)
            if bit:
                sent = jnp.concatenate(list(found.values()), axis=0) if len(found) > 1 else found[0]
                flying["spread", c] = swap(sent, "dp", bit - 1)

    def join(pieces, column, base):
        width = pieces[0].shape[2]
        block = math.gcd(column, width)
        more = [] if base is None else [base]
        return call(
            lambda *refs: join_kernel(n_dp, *refs[: n_dp + 1], refs[-1]),
            [me, *pieces, *more],
            [smem] + [pl.BlockSpec((1, height, block), lambda i: (0, 0, i))] * n_dp + [anywhere] * len(more),
            [
                (
                    shape((n_dp * height, dim), F32),
                    pl.BlockSpec((n_dp * height, block), lambda i: (0, i + column // block)),
                )
            ],
            24,
            "join",
            grid=(width // block,),
            aliases={n_dp + 1: 0} if more else {},
        )[0]

    def finish_weights(landed):
        n_pieces = GROUP // (2 * height)

        def spec(half, k):
            def index(i):
                flat = i * n_pieces + k
                s, d_high = lax.div(flat, n_pairs), lax.rem(flat, n_pairs)
                place = 0
                for at, (axis, bit) in enumerate(w_orders[half]):
                    one = lax.shift_right_logical(s, bit) if axis == "seq" else lax.shift_right_logical(d_high, bit - 1)
                    place = place + lax.bitwise_and(one, 1) * (1 << at)
                return (place, 0, 0)

            return pl.BlockSpec((1, height, dim // 2), index)

        return call(
            functools.partial(weight_kernel, n_pieces),
            [me, *[one for k in range(2) for part in (w_near[k], landed["w", k]) for one in [part] * n_pieces]],
            [smem] + [spec(half, k) for half in range(2) for _ in range(2) for k in range(n_pieces)],
            [(shape((w, hid), BF16), pl.BlockSpec((w, GROUP), lambda i: (0, i))) for w in WIDTHS],
            40,
            "weights",
            grid=(hid // GROUP,),
        )

    def act(first, blocks, base):
        block = 256
        tile = pl.BlockSpec((rows_dev, block), lambda i: (0, i + first))
        more = [] if base is None else [base]
        n_in = 2 * n_parts + 1
        return call(
            lambda *refs: act_kernel(n_parts, *refs[:n_in], refs[-1]),
            [*placed_parts, *weights_t, slope, *more],
            [whole(rows_dev, w) for w in WIDTHS]
            + [pl.BlockSpec((w, block), lambda i: (0, i + first)) for w in WIDTHS]
            + [tile]
            + [anywhere] * len(more),
            [(shape((rows_dev, hid), BF16), tile)],
            60,
            "act",
            grid=(blocks,),
            aliases={n_in: 0} if more else {},
        )[0]

    for _ in range(len(w_bits) - 2):
        landed = boundary("got", "hidden")
        more_weights()
    landed = boundary()
    theirs_t = landed["hidden"]
    [land] = call(
        functools.partial(landing_kernel, n_seq, cap, rows_dev),
        [landed["got"]],
        [whole(n_seq, cap + ID_ROWS, WIDTHS[0])],
        [(shape((rows_dev, slots), BF16), whole(rows_dev, slots))],
        16,
        "landing",
    )
    act_grad = None
    cuts = [(0, 5), (5, 5)]
    assert n_parts == 2
    for c in range(n_parts):
        if c < last:
            flying["got"] = exchange(packed[c])
        if w_names[0] in landed:
            more_weights()
        share(c, place(c))
        advance()
        landed = boundary()
    w_grad = None
    joined = 0
    while joined < n_parts:
        advance()
        spread()
        if w_names[0] in landed:
            more_weights()
            w_last = boundary(*[name for name in flying if name not in w_names])
            weights_t = finish_weights(w_last)
            act_grad = act(*cuts.pop(0), None)
        elif cuts:
            act_grad = act(*cuts.pop(0), act_grad)
        while joined < n_parts and joined in spreads and len(spreads[joined][0]) == n_dp:
            found = spreads[joined][0]
            w_grad = join([found[v] for v in range(n_dp)], sum(WIDTHS[:joined]), w_grad)
            joined += 1
        if flying:
            landed = boundary()
    return act_grad[None], w_grad


def solution(mesh):
    placed = (P("dp", "seq", None), P("dp", "seq"), P("dp", "seq", None), P("seq", None))
    return jax.shard_map(
        local,
        mesh=mesh,
        in_specs=placed,
        out_specs=(P("dp", "seq", None), P("seq", None)),
        check_vma=False,
    )
```

```python
import functools
import math

import jax
import jax.numpy as jnp
from jax import lax
from jax.experimental import pallas as pl
from jax.experimental.pallas import tpu as pltpu
from jax.sharding import PartitionSpec as P

F32, BF16, I32 = jnp.float32, jnp.bfloat16, jnp.int32
MIB = 2**20
WIDTHS = (1024, 768)
ID_BASE = 32
ID_ROWS = 16
GROUP = 640


def dot(a, b, dims=((1,), (0,))):
    return lax.dot_general(a, b, (dims, ((), ())), preferred_element_type=F32)


def params(mib):
    return pltpu.CompilerParams(vmem_limit_bytes=mib * MIB)


def cost(flops, nbytes):
    return pl.CostEstimate(flops=int(flops), bytes_accessed=int(nbytes), transcendentals=0)


def whole(*dims):
    return pl.BlockSpec(dims, lambda *_: (0,) * len(dims))


def reverse(index, bits):
    back = 0
    for bit in range(bits):
        one = lax.bitwise_and(lax.shift_right_logical(index, bit), 1)
        back = back + one * (1 << (bits - 1 - bit))
    return back


def route_kernel(n_seq, cap, rows_dev, map_ref, emb_ref, pick_ref, send_ref):
    targets = map_ref[...]
    groups, lanes = targets.shape
    live = targets >= 0
    safe = jnp.where(live, targets, 0)
    owner = jnp.where(live, lax.div(safe, rows_dev), n_seq)
    members = [(owner == j).astype(F32) for j in range(n_seq)]
    table = jnp.concatenate(members, axis=0).astype(BF16)
    upper = (
        lax.broadcasted_iota(I32, (lanes, lanes), 0) < lax.broadcasted_iota(I32, (lanes, lanes), 1)
    ).astype(F32).astype(BF16)
    inside = dot(table, upper)
    total = n_seq * groups
    row = lax.broadcasted_iota(I32, (total, total), 0)
    col = lax.broadcasted_iota(I32, (total, total), 1)
    earlier = ((lax.div(row, groups) == lax.div(col, groups)) & (col < row)).astype(F32).astype(BF16)
    counts = dot(table, jnp.ones((lanes, lanes), BF16))
    rank_all = inside + dot(earlier, counts.astype(BF16))
    rank = jnp.zeros((groups, lanes), F32)
    for j in range(n_seq):
        rank = rank + members[j] * rank_all[j * groups : (j + 1) * groups]
    slot = jnp.where(live, owner * cap + rank.astype(I32), -1)
    number = jnp.where(live, safe - owner * rows_dev + 1, 0)
    high = lax.div(number, ID_BASE)
    low = (number - high * ID_BASE).astype(F32).astype(BF16)
    high = high.astype(F32).astype(BF16)
    slots = n_seq * cap
    place = lax.broadcasted_iota(I32, (slots, lanes), 0)
    ids = jnp.zeros((ID_ROWS, slots), F32)
    for g in range(groups):
        part = (place == slot[g : g + 1]).astype(F32).astype(BF16)
        pick_ref[:, g * lanes : (g + 1) * lanes] = part
        pair = jnp.concatenate(
            [
                jnp.broadcast_to(high[g : g + 1], (ID_ROWS // 2, lanes)),
                jnp.broadcast_to(low[g : g + 1], (ID_ROWS // 2, lanes)),
            ],
            axis=0,
        )
        ids = ids + dot(pair, part, ((1,), (1,)))
    ids = ids.astype(BF16)
    moved = dot(pick_ref[...], emb_ref[...]).astype(BF16)
    width = emb_ref.shape[1]
    for j in range(n_seq):
        send_ref[j, :cap] = moved[j * cap : (j + 1) * cap]
        digits = ids[:, j * cap : (j + 1) * cap]
        rest = jnp.zeros((ID_ROWS, width - cap), BF16)
        send_ref[j, cap:] = jnp.concatenate([digits, rest], axis=1)


def pack_kernel(n_seq, cap, start, widths, pick_ref, emb_ref, *send_refs):
    first = start
    for send_ref, width in zip(send_refs, widths):
        moved = dot(pick_ref[...], emb_ref[:, first : first + width]).astype(BF16)
        for j in range(n_seq):
            send_ref[j] = moved[j * cap : (j + 1) * cap]
        first += width


def hidden_kernel(height, me_ref, pre_ref, mine_ref, theirs_ref, slope_ref):
    values = pre_ref[...].astype(F32)
    normal_cdf = 0.5 * (1.0 + lax.erf(values * (1.0 / math.sqrt(2.0))))
    density = jnp.exp(-0.5 * values * values) * (1.0 / math.sqrt(2.0 * math.pi))
    slope_ref[...] = normal_cdf + values * density
    hidden = (values * normal_cdf).astype(BF16).T
    even_mine = lax.bitwise_and(me_ref[1], 1) == 0
    for k in range(mine_ref.shape[0] // height):
        even = hidden[2 * k * height : (2 * k + 1) * height]
        odd = hidden[(2 * k + 1) * height : (2 * k + 2) * height]
        mine_ref[k * height : (k + 1) * height] = jnp.where(even_mine, even, odd)
        theirs_ref[k * height : (k + 1) * height] = jnp.where(even_mine, odd, even)


def landing_kernel(n_seq, cap, rows_dev, got_ref, land_ref):
    lows = ID_ROWS // 2
    ids = []
    for i in range(n_seq):
        digits = got_ref[i, cap:].astype(F32)[:, :cap]
        ids.append(digits[0:1] * float(ID_BASE) + digits[lows : lows + 1])
    ids = jnp.concatenate(ids, axis=1).astype(I32) - 1
    slots = ids.shape[1]
    step = 128
    for first in range(0, rows_dev, step):
        row = lax.broadcasted_iota(I32, (step, slots), 0) + first
        land_ref[first : first + step] = (row == ids).astype(F32).astype(BF16)


def place_kernel(n_seq, cap, land_ref, got_ref, placed_ref):
    got = jnp.concatenate([got_ref[i, :cap] for i in range(n_seq)], axis=0)
    placed_ref[...] = dot(land_ref[...], got).astype(BF16)


def share_kernel(n_seq, n_pairs, height, me_ref, mine_ref, theirs_ref, own_ref, other_ref, *refs):
    away_a, keep_a, away_b, keep_b = refs
    step = pl.program_id(0)
    share = dot(mine_ref[...], own_ref[...]) + dot(theirs_ref[...], other_ref[...])
    width = share.shape[1] // 2
    n_far = n_seq // 2
    my_low = lax.bitwise_and(me_ref[0], 1)
    my_pair = lax.shift_right_logical(me_ref[1], 1)
    per_step = mine_ref.shape[0] // (height * n_pairs)
    half = n_pairs // 2

    def block(a, p, column):
        first = (a * n_pairs + p) * height
        return share[first : first + height, column : column + width]

    for a in range(per_step):
        far = (step * per_step + a) // 2
        for p in range(half):
            low, high = block(a, p, 0), block(a, p + half, 0)
            low_mine = my_pair < half
            at = lax.bitwise_xor(p, lax.bitwise_and(my_pair, half - 1)) * n_seq
            at = at + lax.bitwise_xor(a % 2, my_low) * n_far + far
            keep_a[at] = jnp.where(low_mine, low, high)
            away_a[at] = jnp.where(low_mine, high, low).astype(BF16)
    for a in range(0, per_step, 2):
        far = (step * per_step + a) // 2
        for p in range(n_pairs):
            low, high = block(a, p, width), block(a + 1, p, width)
            at = lax.bitwise_xor(p, my_pair) * n_far + far
            keep_b[at] = jnp.where(my_low == 0, low, high)
            away_b[at] = jnp.where(my_low == 0, high, low).astype(BF16)


def add_kernel(keep_a, come_a, keep_b, come_b, send_a, stay_a, send_b, stay_b):
    for keep, come, send, stay in ((keep_a, come_a, send_a, stay_a), (keep_b, come_b, send_b, stay_b)):
        n = stay.shape[0]
        stay[...] = keep[:n] + come[:n].astype(F32)
        send[...] = (keep[n:] + come[n:].astype(F32)).astype(BF16)


def add_join_kernel(keep_a, come_a, keep_b, come_b, out_ref):
    half = keep_a.shape[2]
    out_ref[:, :, :half] = (keep_a[...] + come_a[...].astype(F32)).astype(BF16)
    out_ref[:, :, half:] = (keep_b[...] + come_b[...].astype(F32)).astype(BF16)


def total_kernel(normalizer, come_ref, out_ref):
    total = come_ref[0].astype(F32)
    for k in range(1, come_ref.shape[0]):
        total = total + come_ref[k].astype(F32)
    out_ref[0] = total * normalizer


def weight_kernel(n_pieces, me_ref, *refs):
    refs, out_refs = refs[: 4 * n_pieces], refs[4 * n_pieces :]
    even_mine = lax.bitwise_and(me_ref[1], 1) == 0
    start = 0
    for k in range(2):
        mine_refs, their_refs, refs = refs[:n_pieces], refs[n_pieces : 2 * n_pieces], refs[2 * n_pieces :]
        blocks = []
        for mine, theirs in zip(mine_refs, their_refs):
            blocks.append(jnp.where(even_mine, mine[0], theirs[0]))
            blocks.append(jnp.where(even_mine, theirs[0], mine[0]))
        columns = jnp.concatenate(blocks, axis=0).T
        stop = start + columns.shape[0]
        first = 0
        for out_ref in out_refs:
            low, high = max(start, first), min(stop, first + out_ref.shape[0])
            if low < high:
                out_ref[low - first : high - first] = columns[low - start : high - start]
            first += out_ref.shape[0]
        start = stop


def act_kernel(n_parts, *refs):
    placed_refs, weight_refs, refs = refs[:n_parts], refs[n_parts : 2 * n_parts], refs[2 * n_parts :]
    slope_ref, out_ref = refs
    grad = dot(placed_refs[0][...], weight_refs[0][...])
    for placed_ref, weight_ref in zip(placed_refs[1:], weight_refs[1:]):
        grad = grad + dot(placed_ref[...], weight_ref[...])
    out_ref[...] = (grad * slope_ref[...]).astype(BF16)


def join_kernel(n_dp, me_ref, *refs):
    out_ref = refs[-1]
    height = out_ref.shape[0] // n_dp
    for q in range(n_dp):
        v = lax.bitwise_xor(me_ref[1], q)
        value = refs[0][0]
        for r in range(1, n_dp):
            value = jnp.where(v == r, refs[r][0], value)
        out_ref[q * height : (q + 1) * height] = value


def swap(value, axis, bit):
    size = lax.axis_size(axis)
    return lax.ppermute(value, axis, [(i, i ^ (1 << bit)) for i in range(size)])


def local(emb_grad, image_map, pre_act, w_down):
    n_seq, n_dp = lax.axis_size("seq"), lax.axis_size("dp")
    seq_bits, dp_bits = n_seq.bit_length() - 1, n_dp.bit_length() - 1
    me_s = lax.axis_index("seq").astype(I32)
    me_d = lax.axis_index("dp").astype(I32)
    me = jnp.stack([me_s, me_d])
    tokens, dim = emb_grad.shape[1:]
    rows_dev, hid = pre_act.shape[1:]
    cap = rows_dev // n_seq
    slots = n_seq * cap
    emb, pre = emb_grad[0], pre_act[0]
    n_parts = len(WIDTHS)
    last = n_parts - 1
    height = hid // (n_seq * n_dp)
    n_pairs = n_dp // 2
    kept = n_seq * n_pairs // 2
    normalizer = 1.0 / math.sqrt(n_dp * rows_dev * n_seq)
    smem = pl.BlockSpec(memory_space=pltpu.SMEM)
    anywhere = pl.BlockSpec(memory_space=pl.ANY)
    shape = jax.ShapeDtypeStruct
    cheap = cost(1e6, 1e5)
    clock = None
    flying = {}

    def call(body, operands, in_specs, outs, mib, name, grid=(1,), scratch=(), aliases=None):
        nonlocal clock
        given = [] if clock is None else [clock]

        def timed(*refs):
            n_in = len(operands)
            ins, refs = refs[:n_in], refs[n_in + len(given) :]
            refs[len(outs)][...] = jnp.zeros((8, 128), F32)
            body(*ins, *refs[: len(outs)], *refs[len(outs) + 1 :])

        *results, clock = pl.pallas_call(
            timed,
            grid=grid,
            in_specs=list(in_specs) + [anywhere] * len(given),
            out_specs=[block for _, block in outs] + [whole(8, 128)],
            out_shape=[one for one, _ in outs] + [shape((8, 128), F32)],
            scratch_shapes=list(scratch),
            input_output_aliases=aliases or {},
            compiler_params=params(mib),
            cost_estimate=cheap,
            name=name,
        )(*operands, *given)
        return results

    def order(*values):
        nonlocal clock
        *values, clock = lax.optimization_barrier((*values, clock))
        return values

    def boundary(*beyond):
        names = [n for n in flying if n not in beyond]
        values = order(*[flying.pop(n) for n in names])
        return dict(zip(names, values))

    def exchange(blocks):
        return lax.all_to_all(blocks, "seq", split_axis=0, concat_axis=0, tiled=True)

    w_near = [lax.dynamic_slice(w_down, (me_d * height, 0), (height, dim))[None]]
    w_bits = [("seq", bit) for bit in reversed(range(1, seq_bits))]
    far = [("dp", bit) for bit in reversed(range(1, dp_bits))]
    w_orders = [w_bits + [("seq", 0)] + far, w_bits + far + [("seq", 0)]]
    w_done = [0]
    w_names = (("w", 0), ("w", 1))

    def more_weights():
        at = w_done[0]
        if at:
            for k in range(len(w_near)):
                come = landed["w", k]
                bit = lax.bitwise_and(
                    lax.shift_right_logical(me_s if w_orders[k][at - 1][0] == "seq" else me_d, w_orders[k][at - 1][1]), 1
                )
                halves = jnp.where(bit == 0, w_near[k], come), jnp.where(bit == 0, come, w_near[k])
                w_near[k] = jnp.concatenate(halves, axis=0)
        if at == len(w_bits):
            w_near[:] = [w_near[0][:, :, : dim // 2], w_near[0][:, :, dim // 2 :]]
        for k in range(len(w_near)):
            flying["w", k] = swap(w_near[k], *(w_orders[k][at] if at < len(w_orders[k]) else ("dp", 0)))
        w_done[0] += 1

    more_weights()

    pick, sends = call(
        functools.partial(route_kernel, n_seq, cap, rows_dev),
        [image_map.reshape(tokens // 128, 128), emb],
        [whole(tokens // 128, 128), whole(tokens, WIDTHS[0])],
        [
            (shape((slots, tokens), BF16), whole(slots, tokens)),
            (
                shape((n_seq, cap + ID_ROWS, WIDTHS[0]), BF16),
                whole(n_seq, cap + ID_ROWS, WIDTHS[0]),
            ),
        ],
        60,
        "route",
    )
    landed = boundary()

    flying["got"] = exchange(sends)
    more_weights()
    mine_t, away_t, slope = call(
        functools.partial(hidden_kernel, height),
        [me, pre],
        [smem, pl.BlockSpec((rows_dev, GROUP), lambda i: (0, i))],
        [(shape((hid // 2, rows_dev), BF16), pl.BlockSpec((GROUP // 2, rows_dev), lambda i: (i, 0)))] * 2
        + [(shape((rows_dev, hid), F32), pl.BlockSpec((rows_dev, GROUP), lambda i: (0, i)))],
        60,
        "hidden",
        grid=(hid // GROUP,),
    )
    flying["hidden"] = swap(away_t, "dp", 0)
    rest = WIDTHS[1:]
    packed = call(
        functools.partial(pack_kernel, n_seq, cap, WIDTHS[0], rest),
        [pick, emb],
        [whole(slots, tokens), whole(tokens, dim)],
        [(shape((n_seq, cap, w), BF16), whole(n_seq, cap, w)) for w in rest],
        60,
        "pack",
    )

    far = [("dp", bit) for bit in reversed(range(1, dp_bits))]
    paths = (far + [("seq", 0)], [("seq", 0)] + far)
    columns = [[low + 2 * k for k in range(n_seq // 2)] for low in range(2)]
    placed_parts, sums, done, grads = [], [], [], {}

    def place(c):
        got = landed["got"]
        [placed] = call(
            functools.partial(place_kernel, n_seq, cap),
            [land, got],
            [whole(rows_dev, slots), whole(*got.shape)],
            [(shape((rows_dev, WIDTHS[c]), BF16), whole(rows_dev, WIDTHS[c]))],
            16,
            "place",
        )
        placed_parts.append(placed)
        return swap(placed, "dp", 0)

    def share(c, other):
        width = WIDTHS[c]
        half = width // 2
        *halves, = call(
            functools.partial(share_kernel, n_seq, n_pairs, height),
            [me, mine_t, theirs_t, placed_parts[c], other],
            [smem]
            + [pl.BlockSpec((GROUP // 2, rows_dev), lambda i: (i, 0))] * 2
            + [whole(rows_dev, width)] * 2,
            [(shape((kept, height, half), t), whole(kept, height, half)) for t in (BF16, F32, BF16, F32)],
            40,
            "share",
            grid=(hid // GROUP,),
        )
        sums.append([halves[1], halves[3]])
        done.append(1)
        for k in range(2):
            flying["sum", c, k] = swap(halves[2 * k], *paths[k][0])

    def advance():
        for c in reversed(range(len(sums))):
            names = [name for name in landed if name[0] == "sum" and name[1] == c]
            if not names:
                continue
            come = [landed[name] for name in names]
            at = done[c]
            done[c] += 1
            width = WIDTHS[c]
            if at > len(paths[0]):
                [grads[c]] = call(
                    functools.partial(total_kernel, normalizer),
                    come,
                    [whole(*come[0].shape)],
                    [(shape((1, height, width), F32), whole(1, height, width))],
                    24,
                    "total",
                )
                continue
            terms = [sums[c][0], come[0], sums[c][1], come[1]]
            specs = [whole(*one.shape) for one in terms]
            n = terms[0].shape[0]
            if at < len(paths[0]):
                sizes = (n // 2, height, width // 2)
                results = call(
                    add_kernel,
                    terms,
                    specs,
                    [(shape(sizes, t), whole(*sizes)) for t in (BF16, F32, BF16, F32)],
                    40,
                    "add",
                )
                sums[c] = [results[1], results[3]]
                for k in range(2):
                    flying["sum", c, k] = swap(results[2 * k], *paths[k][at])
            else:
                [sent] = call(
                    add_join_kernel,
                    terms,
                    specs,
                    [(shape((n, height, width), BF16), whole(n, height, width))],
                    40,
                    "add_join",
                )
                flying["sum", c, 0] = lax.all_to_all(
                    sent, "seq", split_axis=0, concat_axis=0, tiled=True, axis_index_groups=columns
                )

    spreads = {}

    def spread():
        for c in range(n_parts):
            if ("spread", c) in landed:
                found, bit = spreads[c]
                come = landed["spread", c]
                for at, v in enumerate(list(found)):
                    found[v + (1 << bit)] = come[at : at + 1]
            elif c not in spreads and c in grads:
                found, bit = {0: grads[c]}, dp_bits
            else:
                continue
            spreads[c] = (found, bit - 1)
            if bit:
                sent = jnp.concatenate(list(found.values()), axis=0) if len(found) > 1 else found[0]
                flying["spread", c] = swap(sent, "dp", bit - 1)

    def join(pieces, column, base):
        width = pieces[0].shape[2]
        block = math.gcd(column, width)
        more = [] if base is None else [base]
        return call(
            lambda *refs: join_kernel(n_dp, *refs[: n_dp + 1], refs[-1]),
            [me, *pieces, *more],
            [smem] + [pl.BlockSpec((1, height, block), lambda i: (0, 0, i))] * n_dp + [anywhere] * len(more),
            [
                (
                    shape((n_dp * height, dim), F32),
                    pl.BlockSpec((n_dp * height, block), lambda i: (0, i + column // block)),
                )
            ],
            24,
            "join",
            grid=(width // block,),
            aliases={n_dp + 1: 0} if more else {},
        )[0]

    def finish_weights(landed):
        n_pieces = GROUP // (2 * height)

        def spec(half, k):
            def index(i):
                flat = i * n_pieces + k
                s, d_high = lax.div(flat, n_pairs), lax.rem(flat, n_pairs)
                place = 0
                for at, (axis, bit) in enumerate(w_orders[half]):
                    one = lax.shift_right_logical(s, bit) if axis == "seq" else lax.shift_right_logical(d_high, bit - 1)
                    place = place + lax.bitwise_and(one, 1) * (1 << at)
                return (place, 0, 0)

            return pl.BlockSpec((1, height, dim // 2), index)

        return call(
            functools.partial(weight_kernel, n_pieces),
            [me, *[one for k in range(2) for part in (w_near[k], landed["w", k]) for one in [part] * n_pieces]],
            [smem] + [spec(half, k) for half in range(2) for _ in range(2) for k in range(n_pieces)],
            [(shape((w, hid), BF16), pl.BlockSpec((w, GROUP), lambda i: (0, i))) for w in WIDTHS],
            40,
            "weights",
            grid=(hid // GROUP,),
        )

    def act(first, blocks, base):
        block = 256
        tile = pl.BlockSpec((rows_dev, block), lambda i: (0, i + first))
        more = [] if base is None else [base]
        n_in = 2 * n_parts + 1
        return call(
            lambda *refs: act_kernel(n_parts, *refs[:n_in], refs[-1]),
            [*placed_parts, *weights_t, slope, *more],
            [whole(rows_dev, w) for w in WIDTHS]
            + [pl.BlockSpec((w, block), lambda i: (0, i + first)) for w in WIDTHS]
            + [tile]
            + [anywhere] * len(more),
            [(shape((rows_dev, hid), BF16), tile)],
            60,
            "act",
            grid=(blocks,),
            aliases={n_in: 0} if more else {},
        )[0]

    for _ in range(len(w_bits) - 2):
        landed = boundary("got", "hidden")
        more_weights()
    landed = boundary()
    theirs_t = landed["hidden"]
    [land] = call(
        functools.partial(landing_kernel, n_seq, cap, rows_dev),
        [landed["got"]],
        [whole(n_seq, cap + ID_ROWS, WIDTHS[0])],
        [(shape((rows_dev, slots), BF16), whole(rows_dev, slots))],
        16,
        "landing",
    )
    act_grad = None
    cuts = [(0, 5), (5, 5)]
    assert n_parts == 2
    for c in range(n_parts):
        if c < last:
            flying["got"] = exchange(packed[c])
        if w_names[0] in landed:
            more_weights()
        share(c, place(c))
        advance()
        landed = boundary()
    w_grad = None
    joined = 0
    while joined < n_parts:
        advance()
        spread()
        if w_names[0] in landed:
            more_weights()
            w_last = boundary(*[name for name in flying if name not in w_names])
            weights_t = finish_weights(w_last)
            act_grad = act(*cuts.pop(0), None)
        elif cuts:
            act_grad = act(*cuts.pop(0), act_grad)
        while joined < n_parts and joined in spreads and len(spreads[joined][0]) == n_dp:
            found = spreads[joined][0]
            w_grad = join([found[v] for v in range(n_dp)], sum(WIDTHS[:joined]), w_grad)
            joined += 1
        if flying:
            landed = boundary()
    return act_grad[None], w_grad


def solution(mesh):
    placed = (P("dp", "seq", None), P("dp", "seq"), P("dp", "seq", None), P("seq", None))
    return jax.shard_map(
        local,
        mesh=mesh,
        in_specs=placed,
        out_specs=(P("dp", "seq", None), P("seq", None)),
        check_vma=False,
    )
```
